32 devices in a mesh: row: 8 (over y, x, core), col: 4 (over z).
Axes of the slice: x: 2, y: 2, z: 4, core: 2. Of those that a mesh axis runs over, the one named last changes fastest.
Arguments:
- head_points: float32 [8, 2, 1024], P(None, None, 'row'), may hold values from 0 to 1
- tail_points: float32 [8, 8192], P(None, 'row'), may hold values from 0 to 1
- eval_points: float32 [8, 4096], P(None, 'col'), may hold values from 0 to 1
- length_scales: float32 [8], replicated, may hold values from 0.5 to 2
- head_factor: float32 [2, 1024, 2, 1024], P(None, 'row', None, 'col'), as said below
- tail_factor: float32 [8192, 2, 1024], P('row', None, 'col'), may hold values from -0.125 to 0.125
Outputs:
- head_solved: float32 [2, 1024, 4096], P(None, 'row', 'col')
- tail_rhs: float32 [8192, 4096], P('row', 'col')
The draws below stay inside these ranges and needn't reach their ends.
Inputs may be any that keep to these rules, and one draw needn't show every extreme that they name: head_factor[p, :, q, :] is zero for q > p; the blocks with p = q are lower triangular with a diagonal between 1 and 2.
All inputs are finite; a program needn't handle non-finite values.
Results may differ from the reference program's by a relative error of at most 0.00011.
Values sent between devices are 32-bit elements; how exact they have to be, the bound alone decides.
A program may use at most 192 MiB of HBM per device.

```python
import math
import jax
import jax.numpy as jnp
from jax import lax

PB = 1024
DIMS = 8
TRAIL = 8192
M = 4096


def draw_head_factor(key, part):
    key_noise = jax.random.fold_in(key, 11)
    key_diag = jax.random.fold_in(key, 23)
    noise = jax.random.normal(key_noise, (2, PB, 2, PB), jnp.float32)
    diagonal = jax.random.uniform(key_diag, (2, PB), jnp.float32, 1.0, 2.0)
    places = jnp.arange(PB)
    lower = (places[:, None] > places[None, :]).astype(jnp.float32)
    panels = jnp.arange(2)
    same = (panels[:, None] == panels[None, :]).astype(jnp.float32)
    below = (panels[:, None] > panels[None, :]).astype(jnp.float32)
    within = same[:, None, :, None] * lower[None, :, None, :] * (0.4 / PB ** 0.5)
    across = below[:, None, :, None] * jnp.ones((1, PB, 1, PB), jnp.float32) * (1.0 / PB ** 0.5)
    identity = same[:, None, :, None] * jnp.eye(PB, dtype=jnp.float32)[None, :, None, :]
    return noise * (within + across) + identity * diagonal[:, :, None, None]


def level_of(key, extent, shards, low, largest):
    loudness = 1.0
    for dim, parts in shards:
        draws = jax.random.uniform(jax.random.fold_in(jax.random.fold_in(key, 6), dim), (parts,), jnp.float32, low / len(shards), largest / len(shards))
        loudness = loudness * jnp.repeat(jnp.exp(draws), extent[dim] // parts).reshape((-1,) + (1,) * (len(extent) - 1 - dim))
    return loudness


def bell_draw(key, extent, width, limit, cuts=(), kind=jnp.bfloat16):
    array = width * jax.random.normal(key, extent, jnp.float32)
    if cuts:
        array = array * level_of(key, extent, cuts, -0.22, 0.18)
    return jnp.clip(array, -limit, limit).astype(kind)


def setup_inputs(seed: int = 0) -> dict:
    key_of = jax.random.split(jax.random.key(seed), 7)
    head_points = jnp.clip(1.0 * jax.random.uniform(key_of[0], (DIMS, 2, PB), jnp.float32) ** level_of(key_of[0], (DIMS, 2, PB), ((2, 8),), -0.2, 0.2), 0.0, 1.0)
    tail_points = jnp.clip(1.0 * jax.random.uniform(key_of[1], (DIMS, TRAIL), jnp.float32) ** level_of(key_of[1], (DIMS, TRAIL), ((1, 8),), -0.2, 0.2), 0.0, 1.0)
    eval_points = jnp.clip(1.0 * jax.random.uniform(key_of[2], (DIMS, M), jnp.float32) ** level_of(key_of[2], (DIMS, M), ((1, 4),), -0.2, 0.2), 0.0, 1.0)
    length_scales = jnp.clip(jnp.exp(jax.random.uniform(key_of[3], (DIMS,), jnp.float32, math.log(0.5), math.log(2.0))), 0.5, 2.0)
    head_factor = draw_head_factor(jax.random.fold_in(key_of[6], 71), 0)
    tail_factor = bell_draw(key_of[5], (TRAIL, 2, PB), (2 * PB) ** -0.5, 0.125, ((0, 8), (2, 4)), jnp.float32)
    return {"head_points": head_points, "tail_points": tail_points, "eval_points": eval_points, "length_scales": length_scales, "head_factor": head_factor, "tail_factor": tail_factor}


def kernel_block(row_points, col_points, length_scales):
    total = jnp.zeros((row_points.shape[1], col_points.shape[1]), jnp.float32)
    for dimension in range(DIMS):
        spread = (row_points[dimension][:, None] - col_points[dimension][None, :]) / length_scales[dimension]
        total = total + spread * spread
    scaled = jnp.sqrt(5.0 * total)
    return (1.0 + scaled + scaled * scaled / 3.0) * jnp.exp(-scaled)

def product(left, right):
    return jnp.dot(left.astype(jnp.float32), right.astype(jnp.float32), precision=lax.Precision.HIGHEST, preferred_element_type=jnp.float32)

def reference(head_points, tail_points, eval_points, length_scales, head_factor, tail_factor):
    first = kernel_block(head_points[:, 0, :], eval_points, length_scales)
    second = kernel_block(head_points[:, 1, :], eval_points, length_scales)
    tail = kernel_block(tail_points, eval_points, length_scales)
    solved_one = jax.scipy.linalg.solve_triangular(head_factor[0, :, 0, :], first, lower=True)
    second_rhs = second - product(head_factor[1, :, 0, :], solved_one)
    solved_two = jax.scipy.linalg.solve_triangular(head_factor[1, :, 1, :], second_rhs, lower=True)
    tail = tail - product(tail_factor[:, 0, :], solved_one)
    tail = tail - product(tail_factor[:, 1, :], solved_two)
    return (jnp.stack([solved_one, solved_two]), tail)
```

```python
import functools

import jax
import jax.numpy as jnp
from jax import lax
from jax.experimental import pallas as pl
from jax.experimental.pallas import tpu as pltpu
from jax.sharding import PartitionSpec as P

MESH = pl.DeviceIdType.MESH
HIGHEST = lax.Precision.HIGHEST
NB = 128


def dot(a, b):
    return jnp.dot(a, b, precision=HIGHEST, preferred_element_type=jnp.float32)


def matern(rows, columns):
    total = jnp.zeros((rows.shape[0], columns.shape[1]), jnp.float32)
    for d in range(columns.shape[0]):
        spread = rows[:, d : d + 1] - columns[d : d + 1, :]
        total = total + spread * spread
    s = jnp.sqrt(5.0 * total)
    return (1.0 + s + s * s * (1.0 / 3.0)) * jnp.exp(-s)


def inverse(block):
    n = block.shape[0]
    i = lax.broadcasted_iota(jnp.int32, (n, n), 0)
    j = lax.broadcasted_iota(jnp.int32, (n, n), 1)
    eye = i == j
    diagonal = jnp.sum(jnp.where(eye, block, 0.0), axis=1, keepdims=True)
    result = jnp.where(eye, 1.0 / diagonal, 0.0)
    size = 1
    while size < n:
        pair = (i // (2 * size) == j // (2 * size)) & ((i // size) % 2 == 1) & ((j // size) % 2 == 0)
        below = jnp.where(pair, block, 0.0)
        result = result - dot(result, dot(below, result))
        size *= 2
    return result


def kernel(
    cols, hp_ref, tp_ref, ev_ref, lh_ref, f_ref, head_out, tail_out,
    hp, l0, l1, x0, x1, rhs, fall, xhi, xlo, own_sem, ex_send, ex_recv, z_send, z_recv,
):
    r = lax.axis_index("row")
    c = lax.axis_index("col")
    sib = r + 1 - 2 * (r % 2)
    across = r + 2 - 4 * ((r // 2) % 2)
    along = r + 4 - 8 * (r // 4)
    corner = across + 4 - 8 * (r // 4)

    def mate(row):
        return row + 1 - 2 * (row % 2)

    own_f = pltpu.make_async_copy(f_ref, fall.at[c], own_sem)
    own_f.start()

    barrier = pltpu.get_barrier_semaphore()
    for row in (sib, across, along):
        pl.semaphore_signal(barrier, inc=1, device_id=(row, c), device_id_type=MESH)

    @pl.when(c > 0)
    def _():
        pl.semaphore_signal(barrier, inc=1, device_id=(r, c - 1), device_id_type=MESH)

    @pl.when(c < cols - 1)
    def _():
        pl.semaphore_signal(barrier, inc=1, device_id=(r, c + 1), device_id_type=MESH)

    hp[r] = hp_ref[...]
    l0[r, c] = lh_ref[0]
    l1[r, c] = lh_ref[1:3]
    pl.semaphore_wait(barrier, 3 + jnp.minimum(c, 1) + jnp.minimum(cols - 1 - c, 1))

    def z_copy(piece, kind, way, t, part, sending):
        shard = (c - t if way == 0 else c + t) if sending else (c - 1 - t if way == 0 else c + 1 + t)
        target = c + 1 if way == 0 else c - 1
        ref = piece(shard, part)
        return pltpu.make_async_remote_copy(
            ref, ref, z_send.at[kind, way, t, part], z_recv.at[kind, way, t, part],
            device_id=(r, target), device_id_type=MESH,
        )

    def z_sends(way, t):
        return (c < cols - 1) & (c - t >= 0) if way == 0 else (c > 0) & (c + t < cols)

    def z_receives(way, t):
        return c - 1 - t >= 0 if way == 0 else c + 1 + t < cols

    def z_start(piece, kind, t, part):
        for way in (0, 1):
            @pl.when(z_sends(way, t))
            def _():
                z_copy(piece, kind, way, t, part, True).start()

    def z_arrive(piece, kind, t, part):
        for way in (0, 1):
            @pl.when(z_receives(way, t))
            def _():
                z_copy(piece, kind, way, t, part, False).wait_recv()

    def z_drain(piece, kind):
        for t in range(cols - 1):
            for part in (0, 1):
                for way in (0, 1):
                    @pl.when(z_sends(way, t))
                    def _():
                        z_copy(piece, kind, way, t, part, True).wait_send()

    def l_piece(shard, part):
        return l0.at[r, shard] if part == 0 else l1.at[r, shard]

    def f_piece(shard, part):
        return fall.at[shard, part]

    def ex_copy(buf, number, k, slot, target, half):
        n = buf.shape[1] // 2
        ref = buf.at[slot] if half is None else buf.at[slot, pl.ds(half * n, n)]
        return pltpu.make_async_remote_copy(
            ref, ref, ex_send.at[number, k], ex_recv.at[number, k], device_id=(target, c), device_id_type=MESH,
        )

    sends = (
        (r, sib, None), (r, across, None), (r, along, None), (across, along, 0), (across, sib, None),
        (along, across, 1), (along, sib, None), (corner, sib, 0), (corner, sib, 1),
    )
    lands = (
        (sib, None), (across, None), (along, None), (corner, 0), (mate(across), None),
        (corner, 1), (mate(along), None), (mate(corner), 0), (mate(corner), 1),
    )

    def ex_start(buf, number, *which):
        for k in which:
            slot, target, half = sends[k]
            ex_copy(buf, number, k, slot, target, half).start()

    def ex_arrive(buf, number, *which):
        for k in which:
            slot, half = lands[k]
            ex_copy(buf, number, k, slot, sib, half).wait_recv()

    def ex_pass(buf, number):
        ex_arrive(buf, number, 1)
        ex_start(buf, number, 3, 4)
        ex_arrive(buf, number, 2)
        ex_start(buf, number, 5, 6)

    def ex_finish(buf, number):
        ex_arrive(buf, number, 3)
        ex_start(buf, number, 7)
        ex_arrive(buf, number, 5)
        ex_start(buf, number, 8)
        ex_arrive(buf, number, 0, 4, 6, 7, 8)
        for k in range(9):
            slot, target, half = sends[k]
            ex_copy(buf, number, k, slot, target, half).wait_send()

    z_start(l_piece, 0, 0, 0)
    z_start(l_piece, 0, 0, 1)
    ex_start(hp, 0, 0, 1, 2)
    for t in range(cols - 1):
        for part in (0, 1):
            z_arrive(l_piece, 0, t, part)
            if t + 1 < cols - 1:
                z_start(l_piece, 0, t + 1, part)
    own_f.wait()
    z_start(f_piece, 1, 0, 0)
    z_start(f_piece, 1, 0, 1)
    z_drain(l_piece, 0)

    group = r // 2
    place = pl.ds(pl.multiple_of((r % 2) * NB, NB), NB)
    l0[r, group, :, place] = inverse(l0[r, group, :, place])
    ex_start(l0, 1, 0, 1, 2)
    l1[r, group, 1, :, place] = inverse(l1[r, group, 1, :, place])
    ex_start(l1, 2, 0, 1, 2)
    ex_pass(hp, 0)
    ex_finish(hp, 0)

    my_columns = ev_ref[:, pl.ds(pl.multiple_of(r * NB, NB), NB)]

    @pl.loop(0, 8)
    def _(b):
        for p in (0, 1):
            rhs[p, pl.ds(pl.multiple_of(b * NB, NB), NB)] = matern(hp[b, p], my_columns)

    ex_pass(l0, 1)
    step = 32

    @pl.loop(0, tail_out.shape[0] // step)
    def _(m):
        rows = pl.ds(pl.multiple_of(m * step, step), step)
        tail_out[rows] = matern(tp_ref[rows], ev_ref[...])

    ex_finish(l0, 1)

    def solve(p, triangle, solved):
        for g in range(4):
            a, b = 2 * g, 2 * g + 1
            xa = dot(triangle(a, g)[:, :NB], rhs[p, a * NB : a * NB + NB])
            right = rhs[p, b * NB : b * NB + NB] - dot(triangle(b, g)[:, :NB], xa)
            xb = dot(triangle(b, g)[:, NB:], right)
            solved[r, a * NB : a * NB + NB] = xa
            solved[r, b * NB : b * NB + NB] = xb
            if g < 3:
                xg = jnp.concatenate([xa, xb], 0)
                for i in range(b + 1, 8):
                    rhs[p, i * NB : i * NB + NB] -= dot(triangle(i, g), xg)

    solve(0, lambda i, g: l0[i, g], x0)
    z_arrive(f_piece, 1, 0, 0)
    z_start(f_piece, 1, 1, 0)
    ex_pass(l1, 2)
    ex_finish(l1, 2)
    ex_start(x0, 3, 0, 1, 2)

    @pl.loop(0, 8)
    def _(i):
        rows = pl.ds(pl.multiple_of(i * NB, NB), NB)
        total = rhs[1, rows]
        for g in range(4):
            total = total - dot(l1[i, g, 0], x0[r, g * 256 : g * 256 + 256])
        rhs[1, rows] = total

    z_arrive(f_piece, 1, 0, 1)
    z_start(f_piece, 1, 1, 1)
    ex_pass(x0, 3)
    solve(1, lambda i, g: l1[i, g, 1], x1)
    ex_start(x1, 4, 0, 1, 2)
    ex_finish(x0, 3)

    def spread_out(p, solved):
        for b in range(8):
            value = solved[b]
            high = value.astype(jnp.bfloat16)
            xhi[p, :, b * NB : b * NB + NB] = high
            xlo[p, :, b * NB : b * NB + NB] = (value - high.astype(jnp.float32)).astype(jnp.bfloat16)
            head_out[p, :, b * NB : b * NB + NB] = solved[b, pl.ds(pl.multiple_of(r * NB, NB), NB)]

    def update(shard, p):
        @pl.loop(0, 4)
        def _(m):
            rows = pl.ds(pl.multiple_of(m * 256, 256), 256)
            deep = pl.ds(pl.multiple_of(shard * 256, 256), 256)
            value = fall[shard, p, rows]
            high = value.astype(jnp.bfloat16)
            low = (value - high.astype(jnp.float32)).astype(jnp.bfloat16)
            right = xhi[p, deep]
            total = jnp.dot(high, right, preferred_element_type=jnp.float32)
            total = total + jnp.dot(low, right, preferred_element_type=jnp.float32)
            total = total + jnp.dot(high, xlo[p, deep], preferred_element_type=jnp.float32)
            tail_out[rows] -= total

    spread_out(0, x0)
    z_arrive(f_piece, 1, 1, 0)
    z_start(f_piece, 1, 2, 0)
    ex_pass(x1, 4)
    ex_finish(x1, 4)
    spread_out(1, x1)
    z_arrive(f_piece, 1, 1, 1)
    z_start(f_piece, 1, 2, 1)

    @pl.loop(0, 2)
    def _(p):
        update(c, p)
        for t in (0, 1):
            for way in (0, 1):
                @pl.when(z_receives(way, t))
                def _():
                    update(c - 1 - t if way == 0 else c + 1 + t, p)

    for p in (0, 1):
        z_arrive(f_piece, 1, 2, p)
        for way in (0, 1):
            @pl.when(z_receives(way, 2))
            def _():
                update(c - 3 if way == 0 else c + 3, p)
    z_drain(f_piece, 1)


def per_device_kernel(cols, head_points, tail_points, eval_points, length_scales, head_factor, tail_factor):
    scale = length_scales[:, None]
    dims = head_points.shape[0]
    hp = jnp.transpose(head_points / scale[:, :, None], (1, 2, 0))
    hp = jnp.pad(hp, ((0, 0), (0, 0), (0, NB - dims)))
    tp = jnp.transpose(tail_points / scale)
    ev = eval_points / scale
    lh = jnp.stack([head_factor[0, :, 0], head_factor[1, :, 0], head_factor[1, :, 1]])
    f = jnp.transpose(tail_factor, (1, 0, 2))
    tail, wide = tail_points.shape[1], eval_points.shape[1]
    vmem = pl.BlockSpec(memory_space=pltpu.VMEM)
    f32 = jnp.float32
    return pl.pallas_call(
        functools.partial(kernel, cols),
        out_shape=(jax.ShapeDtypeStruct((2, NB, wide), f32), jax.ShapeDtypeStruct((tail, wide), f32)),
        in_specs=[vmem, vmem, vmem, vmem, pl.BlockSpec(memory_space=pl.ANY)],
        out_specs=(vmem, vmem),
        scratch_shapes=[
            pltpu.VMEM((8, 2, NB, NB), f32),
            pltpu.VMEM((8, cols, NB, 256), f32),
            pltpu.VMEM((8, cols, 2, NB, 256), f32),
            pltpu.VMEM((8, 1024, NB), f32),
            pltpu.VMEM((8, 1024, NB), f32),
            pltpu.VMEM((2, 1024, NB), f32),
            pltpu.VMEM((cols, 2, tail, 256), f32),
            pltpu.VMEM((2, 1024, wide), jnp.bfloat16),
            pltpu.VMEM((2, 1024, wide), jnp.bfloat16),
            pltpu.SemaphoreType.DMA,
            pltpu.SemaphoreType.DMA((5, 9)),
            pltpu.SemaphoreType.DMA((5, 9)),
            pltpu.SemaphoreType.DMA((2, 2, 3, 2)),
            pltpu.SemaphoreType.DMA((2, 2, 3, 2)),
        ],
        compiler_params=pltpu.CompilerParams(
            collective_id=0, has_side_effects=True, vmem_limit_bytes=60 * 1024 * 1024
        ),
    )(hp, tp, ev, lh, f)


def kernel_block(row_points, col_points, length_scales):
    total = jnp.zeros((row_points.shape[1], col_points.shape[1]), jnp.float32)
    for dimension in range(row_points.shape[0]):
        spread = (row_points[dimension][:, None] - col_points[dimension][None, :]) / length_scales[
            dimension
        ]
        total = total + spread * spread
    scaled = jnp.sqrt(5.0 * total)
    return (1.0 + scaled + scaled * scaled / 3.0) * jnp.exp(-scaled)


def solve_panel(block, right_side):
    band = lax.all_gather(block, "col", axis=1, tiled=True)
    triangle = lax.all_gather(band, "row", axis=0, tiled=True)
    spread = lax.all_to_all(right_side, "row", split_axis=1, concat_axis=0, tiled=True)
    partial_value = jax.scipy.linalg.solve_triangular(triangle, spread, lower=True)
    return lax.all_gather(partial_value, "row", axis=1, tiled=True)


def apply_panel(rows_factor, solved):
    return dot(lax.all_gather(rows_factor, "col", axis=1, tiled=True), solved)


def per_device(head_points, tail_points, eval_points, length_scales, head_factor, tail_factor):
    panel_rows = head_factor.shape[1]
    row_index = lax.axis_index("row")
    second = kernel_block(head_points[:, 1, :], eval_points, length_scales)
    tail = kernel_block(tail_points, eval_points, length_scales)
    first = kernel_block(head_points[:, 0, :], eval_points, length_scales)
    solved_one = solve_panel(head_factor[0, :, 0, :], first)
    update_rows = jnp.concatenate([head_factor[1, :, 0, :], tail_factor[:, 0, :]], 0)
    change = apply_panel(update_rows, solved_one)
    second_rhs = second - change[:panel_rows]
    tail = tail - change[panel_rows:]
    solved_two = solve_panel(head_factor[1, :, 1, :], second_rhs)
    tail = tail - apply_panel(tail_factor[:, 1, :], solved_two)
    local_one = lax.dynamic_slice_in_dim(solved_one, row_index * panel_rows, panel_rows, 0)
    local_two = lax.dynamic_slice_in_dim(solved_two, row_index * panel_rows, panel_rows, 0)
    return (jnp.stack([local_one, local_two]), tail)


def solution(mesh):
    placed = (
        P(None, None, "row"),
        P(None, "row"),
        P(None, "col"),
        P(),
        P(None, "row", None, "col"),
        P("row", None, "col"),
    )
    fits = mesh.shape["row"] == 8 and mesh.shape["col"] == 4
    return jax.shard_map(
        functools.partial(per_device_kernel, mesh.shape["col"]) if fits else per_device,
        mesh=mesh,
        in_specs=placed,
        out_specs=(P(None, "row", "col"), P("row", "col")),
        check_vma=False,
    )
```

```python
import functools

import jax
import jax.numpy as jnp
from jax import lax
from jax.experimental import pallas as pl
from jax.experimental.pallas import tpu as pltpu
from jax.sharding import PartitionSpec as P

MESH = pl.DeviceIdType.MESH
HIGHEST = lax.Precision.HIGHEST
NB = 128
PARTS = 4


def dot(a, b):
    return jnp.dot(a, b, precision=HIGHEST, preferred_element_type=jnp.float32)


def matern(rows, columns, scales):
    total = jnp.zeros((rows.shape[0], columns.shape[1]), jnp.float32)
    for d in range(columns.shape[0]):
        spread = rows[:, d : d + 1] / scales[d] - columns[d : d + 1, :] / scales[d]
        total = total + spread * spread
    s = jnp.sqrt(5.0 * total)
    return (1.0 + s + s * s * (1.0 / 3.0)) * jnp.exp(-s)


def inverse(block):
    n = block.shape[0]
    i = lax.broadcasted_iota(jnp.int32, (n, n), 0)
    j = lax.broadcasted_iota(jnp.int32, (n, n), 1)
    eye = i == j
    diagonal = jnp.sum(jnp.where(eye, block, 0.0), axis=1, keepdims=True)
    result = jnp.where(eye, 1.0 / diagonal, 0.0)
    size = 1
    while size < n:
        pair = (i // (2 * size) == j // (2 * size)) & ((i // size) % 2 == 1) & ((j // size) % 2 == 0)
        below = jnp.where(pair, block, 0.0)
        result = result - dot(result, dot(below, result))
        size *= 2
    return result


def kernel(
    cols, hp_ref, tp_ref, ev_ref, scale_ref, lh_ref, f_ref, head_out, tail_out,
    hp, l0, l1, x0, x1, rhs, fall, xhi, xlo, tail, head, tp,
    own_sem, out_sem, ex_send, ex_recv, z_send, z_recv,
):
    r = lax.axis_index("row")
    c = lax.axis_index("col")
    sib = r + 1 - 2 * (r % 2)
    across = r + 2 - 4 * ((r // 2) % 2)
    along = r + 4 - 8 * (r // 4)
    corner = across + 4 - 8 * (r // 4)

    def mate(row):
        return row + 1 - 2 * (row % 2)

    own_f = pltpu.make_async_copy(f_ref, fall.at[c], own_sem)
    own_f.start()

    barrier = pltpu.get_barrier_semaphore()
    for row in (sib, across, along):
        pl.semaphore_signal(barrier, inc=1, device_id=(row, c), device_id_type=MESH)

    @pl.when(c > 0)
    def _():
        pl.semaphore_signal(barrier, inc=1, device_id=(r, c - 1), device_id_type=MESH)

    @pl.when(c < cols - 1)
    def _():
        pl.semaphore_signal(barrier, inc=1, device_id=(r, c + 1), device_id_type=MESH)

    scales = [scale_ref[d] for d in range(ev_ref.shape[0])]

    def block(p, q):
        return jnp.concatenate([lh_ref[pl.ds(p * 4 * NB + 2 * half + q, NB, stride=4), :] for half in (0, 1)], 1)

    l0[r, c] = block(0, 0)
    l1[r, c, 0] = block(1, 0)
    l1[r, c, 1] = block(1, 1)
    for p in (0, 1):
        hp[r, p] = hp_ref[pl.ds(p, ev_ref.shape[0], stride=2), :]
    pl.semaphore_wait(barrier, 3 + jnp.minimum(c, 1) + jnp.minimum(cols - 1 - c, 1))

    def z_copy(piece, kind, way, t, part, sending):
        shard = (c - t if way == 0 else c + t) if sending else (c - 1 - t if way == 0 else c + 1 + t)
        target = c + 1 if way == 0 else c - 1
        ref = piece(shard, part)
        return pltpu.make_async_remote_copy(
            ref, ref, z_send.at[kind, way, t, part], z_recv.at[kind, way, t, part],
            device_id=(r, target), device_id_type=MESH,
        )

    def z_sends(way, t):
        return (c < cols - 1) & (c - t >= 0) if way == 0 else (c > 0) & (c + t < cols)

    def z_receives(way, t):
        return c - 1 - t >= 0 if way == 0 else c + 1 + t < cols

    def z_start(piece, kind, t, part):
        for way in (0, 1):
            @pl.when(z_sends(way, t))
            def _():
                z_copy(piece, kind, way, t, part, True).start()

    def z_arrive(piece, kind, t, part):
        for way in (0, 1):
            @pl.when(z_receives(way, t))
            def _():
                z_copy(piece, kind, way, t, part, False).wait_recv()

    def z_drain(piece, kind, parts):
        for t in range(cols - 1):
            for part in range(parts):
                for way in (0, 1):
                    @pl.when(z_sends(way, t))
                    def _():
                        z_copy(piece, kind, way, t, part, True).wait_send()

    def l_piece(shard, part):
        return l0.at[r, shard] if part == 0 else l1.at[r, shard]

    def f_piece(shard, part):
        return fall.at[shard, part]

    def ex_copy(buf, number, k, slot, target, half):
        n = buf.shape[1] // 2
        ref = buf.at[slot] if half is None else buf.at[slot, pl.ds(half * n, n)]
        return pltpu.make_async_remote_copy(
            ref, ref, ex_send.at[number, k], ex_recv.at[number, k], device_id=(target, c), device_id_type=MESH,
        )

    sends = (
        (r, sib, None), (r, across, None), (r, along, None), (across, along, 0), (across, sib, None),
        (along, across, 1), (along, sib, None), (corner, sib, 0), (corner, sib, 1),
    )
    lands = (
        (sib, None), (across, None), (along, None), (corner, 0), (mate(across), None),
        (corner, 1), (mate(along), None), (mate(corner), 0), (mate(corner), 1),
    )

    def ex_start(buf, number, *which):
        for k in which:
            slot, target, half = sends[k]
            ex_copy(buf, number, k, slot, target, half).start()

    def ex_arrive(buf, number, *which):
        for k in which:
            slot, half = lands[k]
            ex_copy(buf, number, k, slot, sib, half).wait_recv()

    def ex_pass(buf, number):
        ex_arrive(buf, number, 1)
        ex_start(buf, number, 3, 4)
        ex_arrive(buf, number, 2)
        ex_start(buf, number, 5, 6)

    def ex_finish(buf, number):
        ex_arrive(buf, number, 3)
        ex_start(buf, number, 7)
        ex_arrive(buf, number, 5)
        ex_start(buf, number, 8)
        ex_arrive(buf, number, 0, 4, 6, 7, 8)
        for k in range(9):
            slot, target, half = sends[k]
            ex_copy(buf, number, k, slot, target, half).wait_send()

    z_start(l_piece, 0, 0, 0)
    z_start(l_piece, 0, 0, 1)
    ex_start(hp, 0, 0, 1, 2)
    for t in range(cols - 1):
        for part in (0, 1):
            z_arrive(l_piece, 0, t, part)
            if t + 1 < cols - 1:
                z_start(l_piece, 0, t + 1, part)
    own_f.wait()
    for part in range(PARTS):
        z_start(f_piece, 1, 0, part)
    z_drain(l_piece, 0, 2)

    def pass_on(t, part):
        z_arrive(f_piece, 1, t, part)
        z_start(f_piece, 1, t + 1, part)

    group = r // 2
    place = pl.ds(pl.multiple_of((r % 2) * NB, NB), NB)
    l0[r, group, :, place] = inverse(l0[r, group, :, place])
    ex_start(l0, 1, 0, 1, 2)
    l1[r, group, 1, :, place] = inverse(l1[r, group, 1, :, place])
    ex_start(l1, 2, 0, 1, 2)
    ex_pass(hp, 0)
    ex_finish(hp, 0)

    my_columns = ev_ref[:, pl.ds(pl.multiple_of(r * NB, NB), NB)]

    @pl.loop(0, 8)
    def _(b):
        for p in (0, 1):
            rhs[p, pl.ds(pl.multiple_of(b * NB, NB), NB)] = matern(jnp.transpose(hp[b, p]), my_columns, scales)

    ex_pass(l0, 1)
    step = 32
    for b in range(tp.shape[0] // NB):
        tp[b * NB : b * NB + NB] = jnp.transpose(tp_ref[:, b * NB : b * NB + NB])

    @pl.loop(0, tail.shape[0] // step)
    def _(m):
        rows = pl.ds(pl.multiple_of(m * step, step), step)
        tail[rows] = matern(tp[rows], ev_ref[...], scales)

    ex_finish(l0, 1)
    pass_on(0, 0)

    def solve(p, triangle, solved):
        for g in range(4):
            a, b = 2 * g, 2 * g + 1
            xa = dot(triangle(a, g)[:, :NB], rhs[p, a * NB : a * NB + NB])
            right = rhs[p, b * NB : b * NB + NB] - dot(triangle(b, g)[:, :NB], xa)
            xb = dot(triangle(b, g)[:, NB:], right)
            solved[r, a * NB : a * NB + NB] = xa
            solved[r, b * NB : b * NB + NB] = xb
            if g < 3:
                xg = jnp.concatenate([xa, xb], 0)
                for i in range(b + 1, 8):
                    rhs[p, i * NB : i * NB + NB] -= dot(triangle(i, g), xg)

    solve(0, lambda i, g: l0[i, g], x0)
    pass_on(0, 1)
    ex_pass(l1, 2)
    ex_start(x0, 3, 0, 1, 2)
    pass_on(0, 2)
    ex_finish(l1, 2)

    @pl.loop(0, 8)
    def _(i):
        rows = pl.ds(pl.multiple_of(i * NB, NB), NB)
        total = rhs[1, rows]
        for g in range(4):
            total = total - dot(l1[i, g, 0], x0[r, g * 256 : g * 256 + 256])
        rhs[1, rows] = total

    pass_on(0, 3)
    ex_pass(x0, 3)
    solve(1, lambda i, g: l1[i, g, 1], x1)
    ex_start(x1, 4, 0, 1, 2)
    pass_on(1, 0)
    ex_finish(x0, 3)

    def spread_out(p, solved):
        for b in range(8):
            value = solved[b]
            high = value.astype(jnp.bfloat16)
            xhi[p, :, b * NB : b * NB + NB] = high
            xlo[p, :, b * NB : b * NB + NB] = (value - high.astype(jnp.float32)).astype(jnp.bfloat16)
            head[p, :, b * NB : b * NB + NB] = solved[b, pl.ds(pl.multiple_of(r * NB, NB), NB)]

    def update(shard, part):
        size = fall.shape[2] // 4
        rows = pl.ds(pl.multiple_of(part * size, size), size)
        deep = pl.ds(pl.multiple_of(shard * 256, 256), 256)
        total = tail[rows]
        for q in (0, 1):
            value = jnp.concatenate(
                [fall[shard, part, pl.ds(2 * half + q, size, stride=4), :] for half in (0, 1)], 1
            )
            high = value.astype(jnp.bfloat16)
            low = (value - high.astype(jnp.float32)).astype(jnp.bfloat16)
            right = xhi[q, deep]
            total = total - jnp.dot(high, right, preferred_element_type=jnp.float32)
            total = total - jnp.dot(low, right, preferred_element_type=jnp.float32)
            total = total - jnp.dot(high, xlo[q, deep], preferred_element_type=jnp.float32)
        tail[rows] = total

    def tail_copy(part):
        size = fall.shape[2] // 4
        rows = pl.ds(part * size, size)
        return pltpu.make_async_copy(tail.at[rows], tail_out.at[rows], out_sem.at[part])

    spread_out(0, x0)
    pass_on(1, 1)
    ex_pass(x1, 4)
    pass_on(1, 2)
    ex_finish(x1, 4)
    pass_on(1, 3)
    spread_out(1, x1)
    head_copy = pltpu.make_async_copy(head, head_out, out_sem.at[PARTS])
    head_copy.start()

    @pl.loop(0, PARTS)
    def _(part):
        update(c, part)
        for t in (0, 1):
            for way in (0, 1):
                @pl.when(z_receives(way, t))
                def _():
                    update(c - 1 - t if way == 0 else c + 1 + t, part)

    for part in range(PARTS):
        z_arrive(f_piece, 1, 2, part)

        @pl.when((c == 0) | (c == cols - 1))
        def _():
            update(cols - 1 - c, part)

        tail_copy(part).start()
    z_drain(f_piece, 1, PARTS)
    for part in range(PARTS):
        tail_copy(part).wait()
    head_copy.wait()


def per_device_kernel(cols, head_points, tail_points, eval_points, length_scales, head_factor, tail_factor):
    dims = head_points.shape[0]
    tail, wide = tail_points.shape[1], eval_points.shape[1]

    def by_halves(factor):
        parts = factor.reshape(-1, 2, 2, NB)
        return jnp.transpose(parts, (0, 2, 1, 3)).reshape(-1, NB)

    hp = head_points.reshape(2 * dims, NB)
    lh = by_halves(head_factor)
    f = by_halves(tail_factor).reshape(PARTS, 4 * tail // PARTS, NB)
    vmem = pl.BlockSpec(memory_space=pltpu.VMEM)
    smem = pl.BlockSpec(memory_space=pltpu.SMEM)
    anywhere = pl.BlockSpec(memory_space=pl.ANY)
    f32 = jnp.float32
    return pl.pallas_call(
        functools.partial(kernel, cols),
        out_shape=(jax.ShapeDtypeStruct((2, NB, wide), f32), jax.ShapeDtypeStruct((tail, wide), f32)),
        in_specs=[vmem, vmem, vmem, smem, vmem, anywhere],
        out_specs=(anywhere, anywhere),
        scratch_shapes=[
            pltpu.VMEM((8, 2, dims, NB), f32),
            pltpu.VMEM((8, cols, NB, 256), f32),
            pltpu.VMEM((8, cols, 2, NB, 256), f32),
            pltpu.VMEM((8, 1024, NB), f32),
            pltpu.VMEM((8, 1024, NB), f32),
            pltpu.VMEM((2, 1024, NB), f32),
            pltpu.VMEM((cols, PARTS, 4 * tail // PARTS, NB), f32),
            pltpu.VMEM((2, 1024, wide), jnp.bfloat16),
            pltpu.VMEM((2, 1024, wide), jnp.bfloat16),
            pltpu.VMEM((tail, wide), f32),
            pltpu.VMEM((2, NB, wide), f32),
            pltpu.VMEM((tail, dims), f32),
            pltpu.SemaphoreType.DMA,
            pltpu.SemaphoreType.DMA((PARTS + 1,)),
            pltpu.SemaphoreType.DMA((5, 9)),
            pltpu.SemaphoreType.DMA((5, 9)),
            pltpu.SemaphoreType.DMA((2, 2, 3, PARTS)),
            pltpu.SemaphoreType.DMA((2, 2, 3, PARTS)),
        ],
        compiler_params=pltpu.CompilerParams(
            collective_id=0, has_side_effects=True, vmem_limit_bytes=60 * 1024 * 1024
        ),
    )(hp, tail_points, eval_points, length_scales, lh, f)


def kernel_block(row_points, col_points, length_scales):
    total = jnp.zeros((row_points.shape[1], col_points.shape[1]), jnp.float32)
    for dimension in range(row_points.shape[0]):
        spread = (row_points[dimension][:, None] - col_points[dimension][None, :]) / length_scales[
            dimension
        ]
        total = total + spread * spread
    scaled = jnp.sqrt(5.0 * total)
    return (1.0 + scaled + scaled * scaled / 3.0) * jnp.exp(-scaled)


def solve_panel(block, right_side):
    band = lax.all_gather(block, "col", axis=1, tiled=True)
    triangle = lax.all_gather(band, "row", axis=0, tiled=True)
    spread = lax.all_to_all(right_side, "row", split_axis=1, concat_axis=0, tiled=True)
    partial_value = jax.scipy.linalg.solve_triangular(triangle, spread, lower=True)
    return lax.all_gather(partial_value, "row", axis=1, tiled=True)


def apply_panel(rows_factor, solved):
    return dot(lax.all_gather(rows_factor, "col", axis=1, tiled=True), solved)


def per_device(head_points, tail_points, eval_points, length_scales, head_factor, tail_factor):
    panel_rows = head_factor.shape[1]
    row_index = lax.axis_index("row")
    second = kernel_block(head_points[:, 1, :], eval_points, length_scales)
    tail = kernel_block(tail_points, eval_points, length_scales)
    first = kernel_block(head_points[:, 0, :], eval_points, length_scales)
    solved_one = solve_panel(head_factor[0, :, 0, :], first)
    update_rows = jnp.concatenate([head_factor[1, :, 0, :], tail_factor[:, 0, :]], 0)
    change = apply_panel(update_rows, solved_one)
    second_rhs = second - change[:panel_rows]
    tail = tail - change[panel_rows:]
    solved_two = solve_panel(head_factor[1, :, 1, :], second_rhs)
    tail = tail - apply_panel(tail_factor[:, 1, :], solved_two)
    local_one = lax.dynamic_slice_in_dim(solved_one, row_index * panel_rows, panel_rows, 0)
    local_two = lax.dynamic_slice_in_dim(solved_two, row_index * panel_rows, panel_rows, 0)
    return (jnp.stack([local_one, local_two]), tail)


def solution(mesh):
    placed = (
        P(None, None, "row"),
        P(None, "row"),
        P(None, "col"),
        P(),
        P(None, "row", None, "col"),
        P("row", None, "col"),
    )
    fits = mesh.shape["row"] == 8 and mesh.shape["col"] == 4
    return jax.shard_map(
        functools.partial(per_device_kernel, mesh.shape["col"]) if fits else per_device,
        mesh=mesh,
        in_specs=placed,
        out_specs=(P(None, "row", "col"), P("row", "col")),
        check_vma=False,
    )
```

```python
import functools

import jax
import jax.numpy as jnp
from jax import lax
from jax.experimental import pallas as pl
from jax.experimental.pallas import tpu as pltpu
from jax.sharding import PartitionSpec as P

MESH = pl.DeviceIdType.MESH
HIGHEST = lax.Precision.HIGHEST
NB = 128
PARTS = 4


def dot(a, b):
    return jnp.dot(a, b, precision=HIGHEST, preferred_element_type=jnp.float32)


def matern(rows, columns, scales):
    total = jnp.zeros((rows.shape[0], columns.shape[1]), jnp.float32)
    for d in range(columns.shape[0]):
        spread = rows[:, d : d + 1] / scales[d] - columns[d : d + 1, :] / scales[d]
        total = total + spread * spread
    s = jnp.sqrt(5.0 * total)
    return (1.0 + s + s * s * (1.0 / 3.0)) * jnp.exp(-s)


def inverse(block):
    n = block.shape[0]
    i = lax.broadcasted_iota(jnp.int32, (n, n), 0)
    j = lax.broadcasted_iota(jnp.int32, (n, n), 1)
    eye = i == j
    diagonal = jnp.sum(jnp.where(eye, block, 0.0), axis=1, keepdims=True)
    result = jnp.where(eye, 1.0 / diagonal, 0.0)
    size = 1
    while size < n:
        pair = (i // (2 * size) == j // (2 * size)) & ((i // size) % 2 == 1) & ((j // size) % 2 == 0)
        below = jnp.where(pair, block, 0.0)
        result = result - dot(result, dot(below, result))
        size *= 2
    return result


def kernel(
    cols, hp_ref, tp_ref, ev_ref, scale_ref, lh_ref, f_ref, head_out, tail_out,
    hp, l0, l1, x0, x1, rhs, fall, xhi, xlo, tail, head, tp,
    own_sem, out_sem, ex_send, ex_recv, z_send, z_recv,
):
    r = lax.axis_index("row")
    c = lax.axis_index("col")
    sib = r + 1 - 2 * (r % 2)
    across = r + 2 - 4 * ((r // 2) % 2)
    along = r + 4 - 8 * (r // 4)
    corner = across + 4 - 8 * (r // 4)

    def mate(row):
        return row + 1 - 2 * (row % 2)

    own_f = pltpu.make_async_copy(f_ref, fall.at[c], own_sem)
    own_f.start()

    barrier = pltpu.get_barrier_semaphore()
    for row in (sib, across, along):
        pl.semaphore_signal(barrier, inc=1, device_id=(row, c), device_id_type=MESH)

    @pl.when(c > 0)
    def _():
        pl.semaphore_signal(barrier, inc=1, device_id=(r, c - 1), device_id_type=MESH)

    @pl.when(c < cols - 1)
    def _():
        pl.semaphore_signal(barrier, inc=1, device_id=(r, c + 1), device_id_type=MESH)

    scales = [scale_ref[d] for d in range(ev_ref.shape[0])]

    def block(p, q):
        return jnp.concatenate([lh_ref[pl.ds(p * 4 * NB + 2 * half + q, NB, stride=4), :] for half in (0, 1)], 1)

    l0[r, c] = block(0, 0)
    l1[r, c, 0] = block(1, 0)
    l1[r, c, 1] = block(1, 1)
    for p in (0, 1):
        hp[r, p] = hp_ref[pl.ds(p, ev_ref.shape[0], stride=2), :]
    pl.semaphore_wait(barrier, 3 + jnp.minimum(c, 1) + jnp.minimum(cols - 1 - c, 1))

    def z_copy(piece, kind, way, t, part, sending):
        shard = (c - t if way == 0 else c + t) if sending else (c - 1 - t if way == 0 else c + 1 + t)
        target = c + 1 if way == 0 else c - 1
        ref = piece(shard, part)
        return pltpu.make_async_remote_copy(
            ref, ref, z_send.at[kind, way, t, part], z_recv.at[kind, way, t, part],
            device_id=(r, target), device_id_type=MESH,
        )

    def z_sends(way, t):
        return (c < cols - 1) & (c - t >= 0) if way == 0 else (c > 0) & (c + t < cols)

    def z_receives(way, t):
        return c - 1 - t >= 0 if way == 0 else c + 1 + t < cols

    def z_start(piece, kind, t, part):
        for way in (0, 1):
            @pl.when(z_sends(way, t))
            def _():
                z_copy(piece, kind, way, t, part, True).start()

    def z_arrive(piece, kind, t, part):
        for way in (0, 1):
            @pl.when(z_receives(way, t))
            def _():
                z_copy(piece, kind, way, t, part, False).wait_recv()

    def z_drain(piece, kind, parts):
        for t in range(cols - 1):
            for part in range(parts):
                for way in (0, 1):
                    @pl.when(z_sends(way, t))
                    def _():
                        z_copy(piece, kind, way, t, part, True).wait_send()

    def l_piece(shard, part):
        return l0.at[r, shard] if part == 0 else l1.at[r, shard]

    def f_piece(shard, part):
        return fall.at[shard, part]

    def ex_copy(buf, number, k, slot, target, half):
        n = buf.shape[1] // 2
        ref = buf.at[slot] if half is None else buf.at[slot, pl.ds(half * n, n)]
        return pltpu.make_async_remote_copy(
            ref, ref, ex_send.at[number, k], ex_recv.at[number, k], device_id=(target, c), device_id_type=MESH,
        )

    sends = (
        (r, sib, None), (r, across, None), (r, along, None), (across, along, 0), (across, sib, None),
        (along, across, 1), (along, sib, None), (corner, sib, 0), (corner, sib, 1),
    )
    lands = (
        (sib, None), (across, None), (along, None), (corner, 0), (mate(across), None),
        (corner, 1), (mate(along), None), (mate(corner), 0), (mate(corner), 1),
    )

    def ex_start(buf, number, *which):
        for k in which:
            slot, target, half = sends[k]
            ex_copy(buf, number, k, slot, target, half).start()

    def ex_arrive(buf, number, *which):
        for k in which:
            slot, half = lands[k]
            ex_copy(buf, number, k, slot, sib, half).wait_recv()

    def ex_pass(buf, number):
        ex_arrive(buf, number, 1)
        ex_start(buf, number, 3, 4)
        ex_arrive(buf, number, 2)
        ex_start(buf, number, 5, 6)

    def ex_finish(buf, number):
        ex_arrive(buf, number, 3)
        ex_start(buf, number, 7)
        ex_arrive(buf, number, 5)
        ex_start(buf, number, 8)
        ex_arrive(buf, number, 0, 4, 6, 7, 8)
        for k in range(9):
            slot, target, half = sends[k]
            ex_copy(buf, number, k, slot, target, half).wait_send()

    z_start(l_piece, 0, 0, 0)
    z_start(l_piece, 0, 0, 1)
    ex_start(hp, 0, 0, 1, 2)
    for t in range(cols - 1):
        for part in (0, 1):
            z_arrive(l_piece, 0, t, part)
            if t + 1 < cols - 1:
                z_start(l_piece, 0, t + 1, part)
    own_f.wait()
    for part in range(PARTS):
        z_start(f_piece, 1, 0, part)
    z_drain(l_piece, 0, 2)

    def pass_on(t, part):
        z_arrive(f_piece, 1, t, part)
        z_start(f_piece, 1, t + 1, part)

    group = r // 2
    place = pl.ds(pl.multiple_of((r % 2) * NB, NB), NB)
    l0[r, group, :, place] = inverse(l0[r, group, :, place])
    ex_start(l0, 1, 0, 1, 2)
    l1[r, group, 1, :, place] = inverse(l1[r, group, 1, :, place])
    ex_start(l1, 2, 0, 1, 2)
    ex_pass(hp, 0)
    ex_finish(hp, 0)

    my_columns = ev_ref[:, pl.ds(pl.multiple_of(r * NB, NB), NB)]

    @pl.loop(0, 8)
    def _(b):
        for p in (0, 1):
            rhs[p, pl.ds(pl.multiple_of(b * NB, NB), NB)] = matern(jnp.transpose(hp[b, p]), my_columns, scales)

    ex_pass(l0, 1)
    step = 32
    for b in range(tp.shape[0] // NB):
        tp[b * NB : b * NB + NB] = jnp.transpose(tp_ref[:, b * NB : b * NB + NB])

    @pl.loop(0, tail.shape[0] // step)
    def _(m):
        rows = pl.ds(pl.multiple_of(m * step, step), step)
        tail[rows] = matern(tp[rows], ev_ref[...], scales)

    ex_finish(l0, 1)
    pass_on(0, 0)

    def solve(p, triangle, solved):
        for g in range(4):
            a, b = 2 * g, 2 * g + 1
            xa = dot(triangle(a, g)[:, :NB], rhs[p, a * NB : a * NB + NB])
            right = rhs[p, b * NB : b * NB + NB] - dot(triangle(b, g)[:, :NB], xa)
            xb = dot(triangle(b, g)[:, NB:], right)
            solved[r, a * NB : a * NB + NB] = xa
            solved[r, b * NB : b * NB + NB] = xb
            if g < 3:
                xg = jnp.concatenate([xa, xb], 0)
                for i in range(b + 1, 8):
                    rhs[p, i * NB : i * NB + NB] -= dot(triangle(i, g), xg)

    solve(0, lambda i, g: l0[i, g], x0)
    pass_on(0, 1)
    ex_pass(l1, 2)
    ex_start(x0, 3, 0, 1, 2)
    pass_on(0, 2)
    ex_finish(l1, 2)

    @pl.loop(0, 8)
    def _(i):
        rows = pl.ds(pl.multiple_of(i * NB, NB), NB)
        total = rhs[1, rows]
        for g in range(4):
            total = total - dot(l1[i, g, 0], x0[r, g * 256 : g * 256 + 256])
        rhs[1, rows] = total

    pass_on(0, 3)
    ex_pass(x0, 3)
    solve(1, lambda i, g: l1[i, g, 1], x1)
    ex_start(x1, 4, 0, 1, 2)
    pass_on(1, 0)
    ex_finish(x0, 3)

    def spread_out(p, solved):
        for b in range(8):
            head[p, :, b * NB : b * NB + NB] = solved[b, pl.ds(pl.multiple_of(r * NB, NB), NB)]

    def split(shard):
        deep = pl.ds(pl.multiple_of(shard * 256, 256), 256)
        for q, solved in ((0, x0), (1, x1)):
            for b in range(8):
                value = solved[b, deep]
                high = value.astype(jnp.bfloat16)
                xhi[q, :, b * NB : b * NB + NB] = high
                xlo[q, :, b * NB : b * NB + NB] = (value - high.astype(jnp.float32)).astype(jnp.bfloat16)

    def update(shard, part):
        size = fall.shape[2] // 4
        rows = pl.ds(pl.multiple_of(part * size, size), size)
        total = tail[rows]
        for q in (0, 1):
            value = jnp.concatenate(
                [fall[shard, part, pl.ds(2 * half + q, size, stride=4), :] for half in (0, 1)], 1
            )
            high = value.astype(jnp.bfloat16)
            low = (value - high.astype(jnp.float32)).astype(jnp.bfloat16)
            right = xhi[q]
            total = total - jnp.dot(high, right, preferred_element_type=jnp.float32)
            total = total - jnp.dot(low, right, preferred_element_type=jnp.float32)
            total = total - jnp.dot(high, xlo[q], preferred_element_type=jnp.float32)
        tail[rows] = total

    def tail_copy(part):
        size = fall.shape[2] // 4
        rows = pl.ds(part * size, size)
        return pltpu.make_async_copy(tail.at[rows], tail_out.at[rows], out_sem.at[part])

    spread_out(0, x0)
    pass_on(1, 1)
    ex_pass(x1, 4)
    pass_on(1, 2)
    ex_finish(x1, 4)
    pass_on(1, 3)
    spread_out(1, x1)
    head_copy = pltpu.make_async_copy(head, head_out, out_sem.at[PARTS])
    head_copy.start()

    def update_all(shard):
        split(shard)

        @pl.loop(0, PARTS)
        def _(part):
            update(shard, part)

    update_all(c)
    for t in (0, 1):
        for way in (0, 1):
            @pl.when(z_receives(way, t))
            def _():
                update_all(c - 1 - t if way == 0 else c + 1 + t)

    split(cols - 1 - c)
    for part in range(PARTS):
        z_arrive(f_piece, 1, 2, part)

        @pl.when((c == 0) | (c == cols - 1))
        def _():
            update(cols - 1 - c, part)

        tail_copy(part).start()
    z_drain(f_piece, 1, PARTS)
    for part in range(PARTS):
        tail_copy(part).wait()
    head_copy.wait()


def per_device_kernel(cols, head_points, tail_points, eval_points, length_scales, head_factor, tail_factor):
    dims = head_points.shape[0]
    tail, wide = tail_points.shape[1], eval_points.shape[1]

    def by_halves(factor):
        parts = factor.reshape(-1, 2, 2, NB)
        return jnp.transpose(parts, (0, 2, 1, 3)).reshape(-1, NB)

    hp = head_points.reshape(2 * dims, NB)
    lh = by_halves(head_factor)
    f = by_halves(tail_factor).reshape(PARTS, 4 * tail // PARTS, NB)
    vmem = pl.BlockSpec(memory_space=pltpu.VMEM)
    smem = pl.BlockSpec(memory_space=pltpu.SMEM)
    anywhere = pl.BlockSpec(memory_space=pl.ANY)
    hbm = pl.BlockSpec(memory_space=pltpu.HBM)
    f32 = jnp.float32
    return pl.pallas_call(
        functools.partial(kernel, cols),
        out_shape=(jax.ShapeDtypeStruct((2, NB, wide), f32), jax.ShapeDtypeStruct((tail, wide), f32)),
        in_specs=[vmem, vmem, vmem, smem, vmem, hbm],
        out_specs=(anywhere, anywhere),
        scratch_shapes=[
            pltpu.VMEM((8, 2, dims, NB), f32),
            pltpu.VMEM((8, cols, NB, 256), f32),
            pltpu.VMEM((8, cols, 2, NB, 256), f32),
            pltpu.VMEM((8, 1024, NB), f32),
            pltpu.VMEM((8, 1024, NB), f32),
            pltpu.VMEM((2, 1024, NB), f32),
            pltpu.VMEM((cols, PARTS, 4 * tail // PARTS, NB), f32),
            pltpu.VMEM((2, 256, wide), jnp.bfloat16),
            pltpu.VMEM((2, 256, wide), jnp.bfloat16),
            pltpu.VMEM((tail, wide), f32),
            pltpu.VMEM((2, NB, wide), f32),
            pltpu.VMEM((tail, dims), f32),
            pltpu.SemaphoreType.DMA,
            pltpu.SemaphoreType.DMA((PARTS + 1,)),
            pltpu.SemaphoreType.DMA((5, 9)),
            pltpu.SemaphoreType.DMA((5, 9)),
            pltpu.SemaphoreType.DMA((2, 2, 3, PARTS)),
            pltpu.SemaphoreType.DMA((2, 2, 3, PARTS)),
        ],
        compiler_params=pltpu.CompilerParams(
            collective_id=0, has_side_effects=True, vmem_limit_bytes=44 * 1024 * 1024
        ),
    )(hp, tail_points, eval_points, length_scales, lh, f)


def kernel_block(row_points, col_points, length_scales):
    total = jnp.zeros((row_points.shape[1], col_points.shape[1]), jnp.float32)
    for dimension in range(row_points.shape[0]):
        spread = (row_points[dimension][:, None] - col_points[dimension][None, :]) / length_scales[
            dimension
        ]
        total = total + spread * spread
    scaled = jnp.sqrt(5.0 * total)
    return (1.0 + scaled + scaled * scaled / 3.0) * jnp.exp(-scaled)


def solve_panel(block, right_side):
    band = lax.all_gather(block, "col", axis=1, tiled=True)
    triangle = lax.all_gather(band, "row", axis=0, tiled=True)
    spread = lax.all_to_all(right_side, "row", split_axis=1, concat_axis=0, tiled=True)
    partial_value = jax.scipy.linalg.solve_triangular(triangle, spread, lower=True)
    return lax.all_gather(partial_value, "row", axis=1, tiled=True)


def apply_panel(rows_factor, solved):
    return dot(lax.all_gather(rows_factor, "col", axis=1, tiled=True), solved)


def per_device(head_points, tail_points, eval_points, length_scales, head_factor, tail_factor):
    panel_rows = head_factor.shape[1]
    row_index = lax.axis_index("row")
    second = kernel_block(head_points[:, 1, :], eval_points, length_scales)
    tail = kernel_block(tail_points, eval_points, length_scales)
    first = kernel_block(head_points[:, 0, :], eval_points, length_scales)
    solved_one = solve_panel(head_factor[0, :, 0, :], first)
    update_rows = jnp.concatenate([head_factor[1, :, 0, :], tail_factor[:, 0, :]], 0)
    change = apply_panel(update_rows, solved_one)
    second_rhs = second - change[:panel_rows]
    tail = tail - change[panel_rows:]
    solved_two = solve_panel(head_factor[1, :, 1, :], second_rhs)
    tail = tail - apply_panel(tail_factor[:, 1, :], solved_two)
    local_one = lax.dynamic_slice_in_dim(solved_one, row_index * panel_rows, panel_rows, 0)
    local_two = lax.dynamic_slice_in_dim(solved_two, row_index * panel_rows, panel_rows, 0)
    return (jnp.stack([local_one, local_two]), tail)


def solution(mesh):
    placed = (
        P(None, None, "row"),
        P(None, "row"),
        P(None, "col"),
        P(),
        P(None, "row", None, "col"),
        P("row", None, "col"),
    )
    fits = mesh.shape["row"] == 8 and mesh.shape["col"] == 4
    return jax.shard_map(
        functools.partial(per_device_kernel, mesh.shape["col"]) if fits else per_device,
        mesh=mesh,
        in_specs=placed,
        out_specs=(P(None, "row", "col"), P("row", "col")),
        check_vma=False,
    )
```

```python
import functools

import jax
import jax.numpy as jnp
from jax import lax
from jax.experimental import pallas as pl
from jax.experimental.pallas import tpu as pltpu
from jax.sharding import PartitionSpec as P

MESH = pl.DeviceIdType.MESH
HIGHEST = lax.Precision.HIGHEST
NB = 128
PARTS = 4


def dot(a, b):
    return jnp.dot(a, b, precision=HIGHEST, preferred_element_type=jnp.float32)


def matern(rows, columns, scales):
    total = jnp.zeros((rows.shape[0], columns.shape[1]), jnp.float32)
    for d in range(columns.shape[0]):
        spread = rows[:, d : d + 1] / scales[d] - columns[d : d + 1, :] / scales[d]
        total = total + spread * spread
    s = jnp.sqrt(5.0 * total)
    return (1.0 + s + s * s * (1.0 / 3.0)) * jnp.exp(-s)


def inverse(block):
    n = block.shape[0]
    i = lax.broadcasted_iota(jnp.int32, (n, n), 0)
    j = lax.broadcasted_iota(jnp.int32, (n, n), 1)
    eye = i == j
    diagonal = jnp.sum(jnp.where(eye, block, 0.0), axis=1, keepdims=True)
    result = jnp.where(eye, 1.0 / diagonal, 0.0)
    size = 1
    while size < n:
        pair = (i // (2 * size) == j // (2 * size)) & ((i // size) % 2 == 1) & ((j // size) % 2 == 0)
        below = jnp.where(pair, block, 0.0)
        result = result - dot(result, dot(below, result))
        size *= 2
    return result


def kernel(
    cols, hp_ref, tp_ref, ev_ref, scale_ref, lh_ref, f_ref, head_out, tail_out,
    hp, l0, l1, x0, x1, rhs, fall, xhi, xlo, tail, head, tp,
    own_sem, out_sem, ex_send, ex_recv, z_send, z_recv,
):
    r = lax.axis_index("row")
    c = lax.axis_index("col")
    sib = r + 1 - 2 * (r % 2)
    across = r + 2 - 4 * ((r // 2) % 2)
    along = r + 4 - 8 * (r // 4)
    corner = across + 4 - 8 * (r // 4)

    def mate(row):
        return row + 1 - 2 * (row % 2)

    own_f = pltpu.make_async_copy(f_ref, fall.at[c], own_sem)
    own_f.start()

    barrier = pltpu.get_barrier_semaphore()
    for row in (sib, across, along):
        pl.semaphore_signal(barrier, inc=1, device_id=(row, c), device_id_type=MESH)

    @pl.when(c > 0)
    def _():
        pl.semaphore_signal(barrier, inc=1, device_id=(r, c - 1), device_id_type=MESH)

    @pl.when(c < cols - 1)
    def _():
        pl.semaphore_signal(barrier, inc=1, device_id=(r, c + 1), device_id_type=MESH)

    scales = [scale_ref[d] for d in range(ev_ref.shape[0])]

    def block(p, q):
        return jnp.concatenate([lh_ref[pl.ds(p * 4 * NB + 2 * half + q, NB, stride=4), :] for half in (0, 1)], 1)

    l0[r, c] = block(0, 0)
    l1[r, c, 0] = block(1, 0)
    l1[r, c, 1] = block(1, 1)
    for p in (0, 1):
        hp[r, p] = hp_ref[pl.ds(p, ev_ref.shape[0], stride=2), :]
    pl.semaphore_wait(barrier, 3 + jnp.minimum(c, 1) + jnp.minimum(cols - 1 - c, 1))

    def z_copy(piece, kind, way, t, part, sending):
        shard = (c - t if way == 0 else c + t) if sending else (c - 1 - t if way == 0 else c + 1 + t)
        target = c + 1 if way == 0 else c - 1
        ref = piece(shard, part)
        return pltpu.make_async_remote_copy(
            ref, ref, z_send.at[kind, way, t, part], z_recv.at[kind, way, t, part],
            device_id=(r, target), device_id_type=MESH,
        )

    def z_sends(way, t):
        return (c < cols - 1) & (c - t >= 0) if way == 0 else (c > 0) & (c + t < cols)

    def z_receives(way, t):
        return c - 1 - t >= 0 if way == 0 else c + 1 + t < cols

    def z_start(piece, kind, t, part):
        for way in (0, 1):
            @pl.when(z_sends(way, t))
            def _():
                z_copy(piece, kind, way, t, part, True).start()

    def z_arrive(piece, kind, t, part):
        for way in (0, 1):
            @pl.when(z_receives(way, t))
            def _():
                z_copy(piece, kind, way, t, part, False).wait_recv()

    def z_drain(piece, kind, parts):
        for t in range(cols - 1):
            for part in range(parts):
                for way in (0, 1):
                    @pl.when(z_sends(way, t))
                    def _():
                        z_copy(piece, kind, way, t, part, True).wait_send()

    def l_piece(shard, part):
        return l0.at[r, shard] if part == 0 else l1.at[r, shard]

    def f_piece(shard, part):
        return fall.at[shard, part]

    def ex_copy(buf, number, k, slot, target, half):
        n = buf.shape[1] // 2
        ref = buf.at[slot] if half is None else buf.at[slot, pl.ds(half * n, n)]
        return pltpu.make_async_remote_copy(
            ref, ref, ex_send.at[number, k], ex_recv.at[number, k], device_id=(target, c), device_id_type=MESH,
        )

    sends = (
        (r, sib, None), (r, across, None), (r, along, None), (across, along, 0), (across, sib, None),
        (along, across, 1), (along, sib, None), (corner, sib, 0), (corner, sib, 1),
    )
    lands = (
        (sib, None), (across, None), (along, None), (corner, 0), (mate(across), None),
        (corner, 1), (mate(along), None), (mate(corner), 0), (mate(corner), 1),
    )

    def ex_start(buf, number, *which):
        for k in which:
            slot, target, half = sends[k]
            ex_copy(buf, number, k, slot, target, half).start()

    def ex_arrive(buf, number, *which):
        for k in which:
            slot, half = lands[k]
            ex_copy(buf, number, k, slot, sib, half).wait_recv()

    def ex_pass(buf, number):
        ex_arrive(buf, number, 1)
        ex_start(buf, number, 3, 4)
        ex_arrive(buf, number, 2)
        ex_start(buf, number, 5, 6)

    def ex_finish(buf, number):
        ex_arrive(buf, number, 3)
        ex_start(buf, number, 7)
        ex_arrive(buf, number, 5)
        ex_start(buf, number, 8)
        ex_arrive(buf, number, 0, 4, 6, 7, 8)
        for k in range(9):
            slot, target, half = sends[k]
            ex_copy(buf, number, k, slot, target, half).wait_send()

    z_start(l_piece, 0, 0, 0)
    z_start(l_piece, 0, 0, 1)
    ex_start(hp, 0, 0, 1, 2)
    for t in range(cols - 1):
        for part in (0, 1):
            z_arrive(l_piece, 0, t, part)
            if t + 1 < cols - 1:
                z_start(l_piece, 0, t + 1, part)
    own_f.wait()
    for part in range(PARTS):
        z_start(f_piece, 1, 0, part)
    z_drain(l_piece, 0, 2)

    def pass_on(t, part):
        z_arrive(f_piece, 1, t, part)
        z_start(f_piece, 1, t + 1, part)

    group = r // 2
    place = pl.ds(pl.multiple_of((r % 2) * NB, NB), NB)
    l0[r, group, :, place] = inverse(l0[r, group, :, place])
    ex_start(l0, 1, 0, 1, 2)
    l1[r, group, 1, :, place] = inverse(l1[r, group, 1, :, place])
    ex_start(l1, 2, 0, 1, 2)
    ex_pass(hp, 0)
    ex_finish(hp, 0)

    my_columns = ev_ref[:, pl.ds(pl.multiple_of(r * NB, NB), NB)]

    @pl.loop(0, 8)
    def _(b):
        for p in (0, 1):
            rhs[p, pl.ds(pl.multiple_of(b * NB, NB), NB)] = matern(jnp.transpose(hp[b, p]), my_columns, scales)

    ex_pass(l0, 1)
    step = 32
    for b in range(tp.shape[0] // NB):
        tp[b * NB : b * NB + NB] = jnp.transpose(tp_ref[:, b * NB : b * NB + NB])

    @pl.loop(0, tail.shape[0] // step)
    def _(m):
        rows = pl.ds(pl.multiple_of(m * step, step), step)
        tail[rows] = matern(tp[rows], ev_ref[...], scales)

    ex_finish(l0, 1)
    pass_on(0, 0)

    def solve(p, triangle, solved):
        for g in range(4):
            a, b = 2 * g, 2 * g + 1
            xa = dot(triangle(a, g)[:, :NB], rhs[p, a * NB : a * NB + NB])
            right = rhs[p, b * NB : b * NB + NB] - dot(triangle(b, g)[:, :NB], xa)
            xb = dot(triangle(b, g)[:, NB:], right)
            solved[r, a * NB : a * NB + NB] = xa
            solved[r, b * NB : b * NB + NB] = xb
            if g < 3:
                xg = jnp.concatenate([xa, xb], 0)
                for i in range(b + 1, 8):
                    rhs[p, i * NB : i * NB + NB] -= dot(triangle(i, g), xg)

    solve(0, lambda i, g: l0[i, g], x0)
    pass_on(0, 1)
    ex_pass(l1, 2)
    ex_start(x0, 3, 0, 1, 2)
    pass_on(0, 2)
    ex_finish(l1, 2)

    @pl.loop(0, 8)
    def _(i):
        rows = pl.ds(pl.multiple_of(i * NB, NB), NB)
        total = rhs[1, rows]
        for g in range(4):
            total = total - dot(l1[i, g, 0], x0[r, g * 256 : g * 256 + 256])
        rhs[1, rows] = total

    pass_on(0, 3)
    ex_pass(x0, 3)
    solve(1, lambda i, g: l1[i, g, 1], x1)
    ex_start(x1, 4, 0, 1, 2)
    pass_on(1, 0)
    ex_finish(x0, 3)

    def spread_out(p, solved):
        for b in range(8):
            head[p, :, b * NB : b * NB + NB] = solved[b, pl.ds(pl.multiple_of(r * NB, NB), NB)]

    def split(shard, q):
        deep = pl.ds(pl.multiple_of(shard * 256, 256), 256)
        for b in range(8):
            value = (x0, x1)[q][b, deep]
            high = value.astype(jnp.bfloat16)
            xhi[q, :, b * NB : b * NB + NB] = high
            xlo[q, :, b * NB : b * NB + NB] = (value - high.astype(jnp.float32)).astype(jnp.bfloat16)

    def update(shard, part, *panels):
        size = fall.shape[2] // 4
        rows = pl.ds(pl.multiple_of(part * size, size), size)
        total = tail[rows]
        for q in panels:
            value = jnp.concatenate(
                [fall[shard, part, pl.ds(2 * half + q, size, stride=4), :] for half in (0, 1)], 1
            )
            high = value.astype(jnp.bfloat16)
            low = (value - high.astype(jnp.float32)).astype(jnp.bfloat16)
            right = xhi[q]
            total = total - jnp.dot(high, right, preferred_element_type=jnp.float32)
            total = total - jnp.dot(low, right, preferred_element_type=jnp.float32)
            total = total - jnp.dot(high, xlo[q], preferred_element_type=jnp.float32)
        tail[rows] = total

    def update_all(shard, *panels):
        for q in panels:
            split(shard, q)

        @pl.loop(0, PARTS)
        def _(part):
            update(shard, part, *panels)

    def update_from(t, *panels):
        for way in (0, 1):
            @pl.when(z_receives(way, t))
            def _():
                update_all(c - 1 - t if way == 0 else c + 1 + t, *panels)

    def tail_copy(part):
        size = fall.shape[2] // 4
        rows = pl.ds(part * size, size)
        return pltpu.make_async_copy(tail.at[rows], tail_out.at[rows], out_sem.at[part])

    spread_out(0, x0)
    update_all(c, 0)
    ex_pass(x1, 4)
    pass_on(1, 1)
    update_from(0, 0)
    pass_on(1, 2)
    ex_finish(x1, 4)
    pass_on(1, 3)
    spread_out(1, x1)
    head_copy = pltpu.make_async_copy(head, head_out, out_sem.at[PARTS])
    head_copy.start()
    update_all(c, 1)
    update_from(0, 1)
    update_from(1, 0, 1)
    for q in (0, 1):
        split(cols - 1 - c, q)

    for part in range(PARTS):
        z_arrive(f_piece, 1, 2, part)

        @pl.when((c == 0) | (c == cols - 1))
        def _():
            update(cols - 1 - c, part, 0, 1)

        tail_copy(part).start()
    z_drain(f_piece, 1, PARTS)
    for part in range(PARTS):
        tail_copy(part).wait()
    head_copy.wait()


def per_device_kernel(cols, head_points, tail_points, eval_points, length_scales, head_factor, tail_factor):
    dims = head_points.shape[0]
    tail, wide = tail_points.shape[1], eval_points.shape[1]

    def by_halves(factor):
        parts = factor.reshape(-1, 2, 2, NB)
        return jnp.transpose(parts, (0, 2, 1, 3)).reshape(-1, NB)

    hp = head_points.reshape(2 * dims, NB)
    lh = by_halves(head_factor)
    f = by_halves(tail_factor).reshape(PARTS, 4 * tail // PARTS, NB)
    operands = (hp, tail_points, eval_points, length_scales, lh, f)
    vmem = pl.BlockSpec(memory_space=pltpu.VMEM)
    smem = pl.BlockSpec(memory_space=pltpu.SMEM)
    anywhere = pl.BlockSpec(memory_space=pl.ANY)
    hbm = pl.BlockSpec(memory_space=pltpu.HBM)
    f32 = jnp.float32
    return pl.pallas_call(
        functools.partial(kernel, cols),
        out_shape=(jax.ShapeDtypeStruct((2, NB, wide), f32), jax.ShapeDtypeStruct((tail, wide), f32)),
        in_specs=[vmem, vmem, vmem, smem, vmem, hbm],
        out_specs=(anywhere, anywhere),
        scratch_shapes=[
            pltpu.VMEM((8, 2, dims, NB), f32),
            pltpu.VMEM((8, cols, NB, 256), f32),
            pltpu.VMEM((8, cols, 2, NB, 256), f32),
            pltpu.VMEM((8, 1024, NB), f32),
            pltpu.VMEM((8, 1024, NB), f32),
            pltpu.VMEM((2, 1024, NB), f32),
            pltpu.VMEM((cols, PARTS, 4 * tail // PARTS, NB), f32),
            pltpu.VMEM((2, 256, wide), jnp.bfloat16),
            pltpu.VMEM((2, 256, wide), jnp.bfloat16),
            pltpu.VMEM((tail, wide), f32),
            pltpu.VMEM((2, NB, wide), f32),
            pltpu.VMEM((tail, dims), f32),
            pltpu.SemaphoreType.DMA,
            pltpu.SemaphoreType.DMA((PARTS + 1,)),
            pltpu.SemaphoreType.DMA((5, 9)),
            pltpu.SemaphoreType.DMA((5, 9)),
            pltpu.SemaphoreType.DMA((2, 2, 3, PARTS)),
            pltpu.SemaphoreType.DMA((2, 2, 3, PARTS)),
        ],
        compiler_params=pltpu.CompilerParams(
            collective_id=0, has_side_effects=True, vmem_limit_bytes=44 * 1024 * 1024
        ),
    )(*(pltpu.with_memory_space_constraint(x, pltpu.HBM) for x in operands))


def kernel_block(row_points, col_points, length_scales):
    total = jnp.zeros((row_points.shape[1], col_points.shape[1]), jnp.float32)
    for dimension in range(row_points.shape[0]):
        spread = (row_points[dimension][:, None] - col_points[dimension][None, :]) / length_scales[
            dimension
        ]
        total = total + spread * spread
    scaled = jnp.sqrt(5.0 * total)
    return (1.0 + scaled + scaled * scaled / 3.0) * jnp.exp(-scaled)


def solve_panel(block, right_side):
    band = lax.all_gather(block, "col", axis=1, tiled=True)
    triangle = lax.all_gather(band, "row", axis=0, tiled=True)
    spread = lax.all_to_all(right_side, "row", split_axis=1, concat_axis=0, tiled=True)
    partial_value = jax.scipy.linalg.solve_triangular(triangle, spread, lower=True)
    return lax.all_gather(partial_value, "row", axis=1, tiled=True)


def apply_panel(rows_factor, solved):
    return dot(lax.all_gather(rows_factor, "col", axis=1, tiled=True), solved)


def per_device(head_points, tail_points, eval_points, length_scales, head_factor, tail_factor):
    panel_rows = head_factor.shape[1]
    row_index = lax.axis_index("row")
    second = kernel_block(head_points[:, 1, :], eval_points, length_scales)
    tail = kernel_block(tail_points, eval_points, length_scales)
    first = kernel_block(head_points[:, 0, :], eval_points, length_scales)
    solved_one = solve_panel(head_factor[0, :, 0, :], first)
    update_rows = jnp.concatenate([head_factor[1, :, 0, :], tail_factor[:, 0, :]], 0)
    change = apply_panel(update_rows, solved_one)
    second_rhs = second - change[:panel_rows]
    tail = tail - change[panel_rows:]
    solved_two = solve_panel(head_factor[1, :, 1, :], second_rhs)
    tail = tail - apply_panel(tail_factor[:, 1, :], solved_two)
    local_one = lax.dynamic_slice_in_dim(solved_one, row_index * panel_rows, panel_rows, 0)
    local_two = lax.dynamic_slice_in_dim(solved_two, row_index * panel_rows, panel_rows, 0)
    return (jnp.stack([local_one, local_two]), tail)


def solution(mesh):
    placed = (
        P(None, None, "row"),
        P(None, "row"),
        P(None, "col"),
        P(),
        P(None, "row", None, "col"),
        P("row", None, "col"),
    )
    fits = mesh.shape["row"] == 8 and mesh.shape["col"] == 4
    return jax.shard_map(
        functools.partial(per_device_kernel, mesh.shape["col"]) if fits else per_device,
        mesh=mesh,
        in_specs=placed,
        out_specs=(P(None, "row", "col"), P("row", "col")),
        check_vma=False,
    )
```

```python
import functools

import jax
import jax.numpy as jnp
from jax import lax
from jax.experimental import pallas as pl
from jax.experimental.pallas import tpu as pltpu
from jax.sharding import PartitionSpec as P

MESH = pl.DeviceIdType.MESH
HIGHEST = lax.Precision.HIGHEST
NB = 128
PARTS = 4


def dot(a, b):
    return jnp.dot(a, b, precision=HIGHEST, preferred_element_type=jnp.float32)


def matern(rows, columns, scales):
    total = jnp.zeros((rows.shape[0], columns.shape[1]), jnp.float32)
    for d in range(columns.shape[0]):
        spread = rows[:, d : d + 1] / scales[d] - columns[d : d + 1, :] / scales[d]
        total = total + spread * spread
    s = jnp.sqrt(5.0 * total)
    return (1.0 + s + s * s * (1.0 / 3.0)) * jnp.exp(-s)


def inverse(block):
    n = block.shape[0]
    i = lax.broadcasted_iota(jnp.int32, (n, n), 0)
    j = lax.broadcasted_iota(jnp.int32, (n, n), 1)
    eye = i == j
    diagonal = jnp.sum(jnp.where(eye, block, 0.0), axis=1, keepdims=True)
    result = jnp.where(eye, 1.0 / diagonal, 0.0)
    size = 1
    while size < n:
        pair = (i // (2 * size) == j // (2 * size)) & ((i // size) % 2 == 1) & ((j // size) % 2 == 0)
        below = jnp.where(pair, block, 0.0)
        result = result - dot(result, dot(below, result))
        size *= 2
    return result


def kernel(
    cols, hp_ref, tp_ref, ev_ref, scale_ref, lh_ref, f_ref, head_out, tail_out,
    hp, l0, l1, x0, x1, rhs, fall, xhi, xlo, tail, head, tp,
    own_sem, out_sem, ex_send, ex_recv, z_send, z_recv,
):
    r = lax.axis_index("row")
    c = lax.axis_index("col")
    sib = r + 1 - 2 * (r % 2)
    across = r + 2 - 4 * ((r // 2) % 2)
    along = r + 4 - 8 * (r // 4)
    corner = across + 4 - 8 * (r // 4)

    def mate(row):
        return row + 1 - 2 * (row % 2)

    own_f = pltpu.make_async_copy(f_ref, fall.at[c], own_sem)
    own_f.start()

    barrier = pltpu.get_barrier_semaphore()
    for row in (sib, across, along):
        pl.semaphore_signal(barrier, inc=1, device_id=(row, c), device_id_type=MESH)

    @pl.when(c > 0)
    def _():
        pl.semaphore_signal(barrier, inc=1, device_id=(r, c - 1), device_id_type=MESH)

    @pl.when(c < cols - 1)
    def _():
        pl.semaphore_signal(barrier, inc=1, device_id=(r, c + 1), device_id_type=MESH)

    scales = [scale_ref[d] for d in range(ev_ref.shape[0])]

    def block(p, q):
        return jnp.concatenate([lh_ref[pl.ds(p * 4 * NB + 2 * half + q, NB, stride=4), :] for half in (0, 1)], 1)

    l0[r, c] = block(0, 0)
    l1[r, c, 0] = block(1, 0)
    l1[r, c, 1] = block(1, 1)
    for p in (0, 1):
        hp[r, p] = hp_ref[pl.ds(p, ev_ref.shape[0], stride=2), :]
    pl.semaphore_wait(barrier, 3 + jnp.minimum(c, 1) + jnp.minimum(cols - 1 - c, 1))

    def z_copy(piece, kind, way, t, part, sending):
        shard = (c - t if way == 0 else c + t) if sending else (c - 1 - t if way == 0 else c + 1 + t)
        target = c + 1 if way == 0 else c - 1
        ref = piece(shard, part)
        return pltpu.make_async_remote_copy(
            ref, ref, z_send.at[kind, way, t, part], z_recv.at[kind, way, t, part],
            device_id=(r, target), device_id_type=MESH,
        )

    def z_sends(way, t):
        return (c < cols - 1) & (c - t >= 0) if way == 0 else (c > 0) & (c + t < cols)

    def z_receives(way, t):
        return c - 1 - t >= 0 if way == 0 else c + 1 + t < cols

    def z_start(piece, kind, t, part):
        for way in (0, 1):
            @pl.when(z_sends(way, t))
            def _():
                z_copy(piece, kind, way, t, part, True).start()

    def z_arrive(piece, kind, t, part):
        for way in (0, 1):
            @pl.when(z_receives(way, t))
            def _():
                z_copy(piece, kind, way, t, part, False).wait_recv()

    def z_drain(piece, kind, parts):
        for t in range(cols - 1):
            for part in range(parts):
                for way in (0, 1):
                    @pl.when(z_sends(way, t))
                    def _():
                        z_copy(piece, kind, way, t, part, True).wait_send()

    def l_piece(shard, part):
        return l0.at[r, shard] if part == 0 else l1.at[r, shard]

    def f_piece(shard, part):
        return fall.at[shard, part]

    def ex_copy(buf, number, k, slot, target, half):
        n = buf.shape[1] // 2
        ref = buf.at[slot] if half is None else buf.at[slot, pl.ds(half * n, n)]
        return pltpu.make_async_remote_copy(
            ref, ref, ex_send.at[number, k], ex_recv.at[number, k], device_id=(target, c), device_id_type=MESH,
        )

    sends = (
        (r, sib, None), (r, across, None), (r, along, None), (across, along, 0), (across, sib, None),
        (along, across, 1), (along, sib, None), (corner, sib, 0), (corner, sib, 1),
    )
    lands = (
        (sib, None), (across, None), (along, None), (corner, 0), (mate(across), None),
        (corner, 1), (mate(along), None), (mate(corner), 0), (mate(corner), 1),
    )

    def ex_start(buf, number, *which):
        for k in which:
            slot, target, half = sends[k]
            ex_copy(buf, number, k, slot, target, half).start()

    def ex_arrive(buf, number, *which):
        for k in which:
            slot, half = lands[k]
            ex_copy(buf, number, k, slot, sib, half).wait_recv()

    def ex_pass(buf, number):
        ex_arrive(buf, number, 1)
        ex_start(buf, number, 3, 4)
        ex_arrive(buf, number, 2)
        ex_start(buf, number, 5, 6)

    def ex_finish(buf, number):
        ex_arrive(buf, number, 3)
        ex_start(buf, number, 7)
        ex_arrive(buf, number, 5)
        ex_start(buf, number, 8)
        ex_arrive(buf, number, 0, 4, 6, 7, 8)
        for k in range(9):
            slot, target, half = sends[k]
            ex_copy(buf, number, k, slot, target, half).wait_send()

    z_start(l_piece, 0, 0, 0)
    z_start(l_piece, 0, 0, 1)
    ex_start(hp, 0, 0, 1, 2)
    for t in range(cols - 1):
        for part in (0, 1):
            z_arrive(l_piece, 0, t, part)
            if t + 1 < cols - 1:
                z_start(l_piece, 0, t + 1, part)
    own_f.wait()
    for part in range(PARTS):
        z_start(f_piece, 1, 0, part)
    z_drain(l_piece, 0, 2)

    def pass_on(t, part):
        z_arrive(f_piece, 1, t, part)
        z_start(f_piece, 1, t + 1, part)

    group = r // 2
    place = pl.ds(pl.multiple_of((r % 2) * NB, NB), NB)
    l0[r, group, :, place] = inverse(l0[r, group, :, place])
    ex_start(l0, 1, 0, 1, 2)
    l1[r, group, 1, :, place] = inverse(l1[r, group, 1, :, place])
    ex_start(l1, 2, 0, 1, 2)
    ex_pass(hp, 0)
    ex_finish(hp, 0)

    my_columns = ev_ref[:, pl.ds(pl.multiple_of(r * NB, NB), NB)]

    @pl.loop(0, 8)
    def _(b):
        for p in (0, 1):
            rhs[p, pl.ds(pl.multiple_of(b * NB, NB), NB)] = matern(jnp.transpose(hp[b, p]), my_columns, scales)

    ex_pass(l0, 1)
    step = 32
    for b in range(tp.shape[0] // NB):
        tp[b * NB : b * NB + NB] = jnp.transpose(tp_ref[:, b * NB : b * NB + NB])

    @pl.loop(0, tail.shape[0] // step)
    def _(m):
        rows = pl.ds(pl.multiple_of(m * step, step), step)
        tail[rows] = matern(tp[rows], ev_ref[...], scales)

    ex_finish(l0, 1)
    pass_on(0, 0)

    def solve(p, triangle, solved):
        for g in range(4):
            a, b = 2 * g, 2 * g + 1
            xa = dot(triangle(a, g)[:, :NB], rhs[p, a * NB : a * NB + NB])
            right = rhs[p, b * NB : b * NB + NB] - dot(triangle(b, g)[:, :NB], xa)
            xb = dot(triangle(b, g)[:, NB:], right)
            solved[r, a * NB : a * NB + NB] = xa
            solved[r, b * NB : b * NB + NB] = xb
            if g < 3:
                xg = jnp.concatenate([xa, xb], 0)
                for i in range(b + 1, 8):
                    rhs[p, i * NB : i * NB + NB] -= dot(triangle(i, g), xg)

    solve(0, lambda i, g: l0[i, g], x0)
    pass_on(0, 1)
    ex_pass(l1, 2)
    ex_start(x0, 3, 0, 1, 2)
    pass_on(0, 2)
    ex_finish(l1, 2)

    @pl.loop(0, 8)
    def _(i):
        rows = pl.ds(pl.multiple_of(i * NB, NB), NB)
        total = rhs[1, rows]
        for g in range(4):
            total = total - dot(l1[i, g, 0], x0[r, g * 256 : g * 256 + 256])
        rhs[1, rows] = total

    pass_on(0, 3)
    ex_pass(x0, 3)
    pass_on(1, 0)
    solve(1, lambda i, g: l1[i, g, 1], x1)
    ex_start(x1, 4, 0, 1, 2)
    pass_on(1, 1)
    ex_finish(x0, 3)

    def spread_out(p, solved):
        for b in range(8):
            head[p, :, b * NB : b * NB + NB] = solved[b, pl.ds(pl.multiple_of(r * NB, NB), NB)]

    def split(shard, q):
        deep = pl.ds(pl.multiple_of(shard * 256, 256), 256)
        for b in range(8):
            value = (x0, x1)[q][b, deep]
            high = value.astype(jnp.bfloat16)
            xhi[q, :, b * NB : b * NB + NB] = high
            xlo[q, :, b * NB : b * NB + NB] = (value - high.astype(jnp.float32)).astype(jnp.bfloat16)

    def update(shard, part, *panels):
        size = fall.shape[2] // 4
        rows = pl.ds(pl.multiple_of(part * size, size), size)
        total = tail[rows]
        for q in panels:
            value = jnp.concatenate(
                [fall[shard, part, pl.ds(2 * half + q, size, stride=4), :] for half in (0, 1)], 1
            )
            high = value.astype(jnp.bfloat16)
            low = (value - high.astype(jnp.float32)).astype(jnp.bfloat16)
            right = xhi[q]
            total = total - jnp.dot(high, right, preferred_element_type=jnp.float32)
            total = total - jnp.dot(low, right, preferred_element_type=jnp.float32)
            total = total - jnp.dot(high, xlo[q], preferred_element_type=jnp.float32)
        tail[rows] = total

    def update_all(shard, *panels):
        for q in panels:
            split(shard, q)

        @pl.loop(0, PARTS)
        def _(part):
            update(shard, part, *panels)

    def update_from(t, *panels):
        for way in (0, 1):
            @pl.when(z_receives(way, t))
            def _():
                update_all(c - 1 - t if way == 0 else c + 1 + t, *panels)

    def tail_copy(part):
        size = fall.shape[2] // 4
        rows = pl.ds(part * size, size)
        return pltpu.make_async_copy(tail.at[rows], tail_out.at[rows], out_sem.at[part])

    spread_out(0, x0)
    pass_on(1, 2)
    update_all(c, 0)
    ex_pass(x1, 4)
    pass_on(1, 3)
    update_from(0, 0)
    ex_finish(x1, 4)
    spread_out(1, x1)
    head_copy = pltpu.make_async_copy(head, head_out, out_sem.at[PARTS])
    head_copy.start()
    update_all(c, 1)
    update_from(0, 1)
    update_from(1, 0, 1)
    for q in (0, 1):
        split(cols - 1 - c, q)

    for part in range(PARTS):
        z_arrive(f_piece, 1, 2, part)

        @pl.when((c == 0) | (c == cols - 1))
        def _():
            update(cols - 1 - c, part, 0, 1)

        tail_copy(part).start()
    z_drain(f_piece, 1, PARTS)
    for part in range(PARTS):
        tail_copy(part).wait()
    head_copy.wait()


def per_device_kernel(cols, head_points, tail_points, eval_points, length_scales, head_factor, tail_factor):
    dims = head_points.shape[0]
    tail, wide = tail_points.shape[1], eval_points.shape[1]

    def by_halves(factor):
        parts = factor.reshape(-1, 2, 2, NB)
        return jnp.transpose(parts, (0, 2, 1, 3)).reshape(-1, NB)

    hp = head_points.reshape(2 * dims, NB)
    lh = by_halves(head_factor)
    f = by_halves(tail_factor).reshape(PARTS, 4 * tail // PARTS, NB)
    operands = (hp, tail_points, eval_points, length_scales, lh, f)
    vmem = pl.BlockSpec(memory_space=pltpu.VMEM)
    smem = pl.BlockSpec(memory_space=pltpu.SMEM)
    anywhere = pl.BlockSpec(memory_space=pl.ANY)
    hbm = pl.BlockSpec(memory_space=pltpu.HBM)
    f32 = jnp.float32
    return pl.pallas_call(
        functools.partial(kernel, cols),
        out_shape=(jax.ShapeDtypeStruct((2, NB, wide), f32), jax.ShapeDtypeStruct((tail, wide), f32)),
        in_specs=[vmem, vmem, vmem, smem, vmem, hbm],
        out_specs=(anywhere, anywhere),
        scratch_shapes=[
            pltpu.VMEM((8, 2, dims, NB), f32),
            pltpu.VMEM((8, cols, NB, 256), f32),
            pltpu.VMEM((8, cols, 2, NB, 256), f32),
            pltpu.VMEM((8, 1024, NB), f32),
            pltpu.VMEM((8, 1024, NB), f32),
            pltpu.VMEM((2, 1024, NB), f32),
            pltpu.VMEM((cols, PARTS, 4 * tail // PARTS, NB), f32),
            pltpu.VMEM((2, 256, wide), jnp.bfloat16),
            pltpu.VMEM((2, 256, wide), jnp.bfloat16),
            pltpu.VMEM((tail, wide), f32),
            pltpu.VMEM((2, NB, wide), f32),
            pltpu.VMEM((tail, dims), f32),
            pltpu.SemaphoreType.DMA,
            pltpu.SemaphoreType.DMA((PARTS + 1,)),
            pltpu.SemaphoreType.DMA((5, 9)),
            pltpu.SemaphoreType.DMA((5, 9)),
            pltpu.SemaphoreType.DMA((2, 2, 3, PARTS)),
            pltpu.SemaphoreType.DMA((2, 2, 3, PARTS)),
        ],
        compiler_params=pltpu.CompilerParams(
            collective_id=0, has_side_effects=True, vmem_limit_bytes=44 * 1024 * 1024
        ),
    )(*(pltpu.with_memory_space_constraint(x, pltpu.HBM) for x in operands))


def kernel_block(row_points, col_points, length_scales):
    total = jnp.zeros((row_points.shape[1], col_points.shape[1]), jnp.float32)
    for dimension in range(row_points.shape[0]):
        spread = (row_points[dimension][:, None] - col_points[dimension][None, :]) / length_scales[
            dimension
        ]
        total = total + spread * spread
    scaled = jnp.sqrt(5.0 * total)
    return (1.0 + scaled + scaled * scaled / 3.0) * jnp.exp(-scaled)


def solve_panel(block, right_side):
    band = lax.all_gather(block, "col", axis=1, tiled=True)
    triangle = lax.all_gather(band, "row", axis=0, tiled=True)
    spread = lax.all_to_all(right_side, "row", split_axis=1, concat_axis=0, tiled=True)
    partial_value = jax.scipy.linalg.solve_triangular(triangle, spread, lower=True)
    return lax.all_gather(partial_value, "row", axis=1, tiled=True)


def apply_panel(rows_factor, solved):
    return dot(lax.all_gather(rows_factor, "col", axis=1, tiled=True), solved)


def per_device(head_points, tail_points, eval_points, length_scales, head_factor, tail_factor):
    panel_rows = head_factor.shape[1]
    row_index = lax.axis_index("row")
    second = kernel_block(head_points[:, 1, :], eval_points, length_scales)
    tail = kernel_block(tail_points, eval_points, length_scales)
    first = kernel_block(head_points[:, 0, :], eval_points, length_scales)
    solved_one = solve_panel(head_factor[0, :, 0, :], first)
    update_rows = jnp.concatenate([head_factor[1, :, 0, :], tail_factor[:, 0, :]], 0)
    change = apply_panel(update_rows, solved_one)
    second_rhs = second - change[:panel_rows]
    tail = tail - change[panel_rows:]
    solved_two = solve_panel(head_factor[1, :, 1, :], second_rhs)
    tail = tail - apply_panel(tail_factor[:, 1, :], solved_two)
    local_one = lax.dynamic_slice_in_dim(solved_one, row_index * panel_rows, panel_rows, 0)
    local_two = lax.dynamic_slice_in_dim(solved_two, row_index * panel_rows, panel_rows, 0)
    return (jnp.stack([local_one, local_two]), tail)


def solution(mesh):
    placed = (
        P(None, None, "row"),
        P(None, "row"),
        P(None, "col"),
        P(),
        P(None, "row", None, "col"),
        P("row", None, "col"),
    )
    fits = mesh.shape["row"] == 8 and mesh.shape["col"] == 4
    return jax.shard_map(
        functools.partial(per_device_kernel, mesh.shape["col"]) if fits else per_device,
        mesh=mesh,
        in_specs=placed,
        out_specs=(P(None, "row", "col"), P("row", "col")),
        check_vma=False,
    )
```
